32 devices in a mesh: section: 2 (over y), dp: 4 (over z), tower: 4 (over x, core).
Axes of the slice: x: 2, y: 2, z: 4, core: 2. Of those that a mesh axis runs over, the one named last changes fastest.
Arguments:
- stream: bfloat16 [2, 256, 4096], P(None, 'tower', 'dp'), may hold values from -17.5 to 17.5
- routes: int32 [2, 256, 1], P(None, 'tower'), may hold values from 0 to 3; in each aligned block of 64 rows (0 to 63, 64 to 127, ..., all dimensions but the last counted through in order) at most 32 rows name the same one
- tower_gain: float32 [2, 4, 4096], P('section', 'tower'), may hold values from 0.1 to 1.9
- qkv_weight: bfloat16 [2, 4, 4096, 4, 3, 128], P('section', 'tower', None, 'dp'), may hold values from -1 to 1
- out_weight: bfloat16 [2, 4, 4, 128, 4096], P('section', 'tower', None, None, 'dp'), may hold values from -0.25 to 0.25
Outputs:
- section_out: bfloat16 [2, 2, 256, 4096], P('section', None, 'tower', 'dp')
The draws below stay inside these ranges and needn't reach their ends.
Inputs may be any that keep to these rules, and one draw needn't show every extreme that they name: `routes`: in each micro-batch at most 32 of the 64 rows of one tower device name the same tower group, and every draw reaches 32.
All inputs are finite; a program needn't handle non-finite values.
Results may differ from the reference program's by a relative error of at most 0.022.
Values may be sent and summed in bfloat16 or wider, within the bound.
A program may use at most 64 MiB of HBM per device.

```python
import math
import jax
import jax.numpy as jnp
import numpy as np
from jax import lax

D = 4096
HD = 128
HEADS = 4
TOKM = 64
MB = 2
SEQ = 256
N_SECTION = 2
N_TOWER = 4


def draw_stream(key, part):
    key = jax.random.fold_in(key, 11)
    shape = (MB, SEQ, D)
    base = jnp.clip(jax.random.normal(key, shape, jnp.float32), -6.0, 6.0)
    return base.astype(jnp.bfloat16)


def draw_qkv_weight(key, part):
    key = jax.random.fold_in(key, 23)
    shape = (N_SECTION, N_TOWER, D, HEADS, 3, HD)
    base = jnp.clip(jax.random.normal(key, shape, jnp.float32), -6.0, 6.0) * D ** (-0.5)
    return jnp.clip(base, -1.0, 1.0).astype(jnp.bfloat16)


def steps_of(key, dims, cuts, least, high):
    gain = 1.0
    for axis_at, parts in cuts:
        steps = jax.random.uniform(jax.random.fold_in(jax.random.fold_in(key, 6), axis_at), (parts,), jnp.float32, least / len(cuts), high / len(cuts))
        gain = gain * jnp.repeat(jnp.exp(steps), dims[axis_at] // parts).reshape((-1,) + (1,) * (len(dims) - 1 - axis_at))
    return gain


def assign_block(key, own, number, rows, count, top, reach, skew):
    ranking = jax.random.permutation(key, count)
    heavy_load, common = load_shares(count, rows * top, reach, skew, True), load_shares(count, rows * top, reach, skew, False)
    places = jnp.arange(count)

    def named(sizes, turn):
        used = int((sizes > 0).sum())
        fixed = max(1, used // 4)
        passed = fixed + (places - fixed + turn * (used - fixed)) % max(1, count - fixed)
        return jnp.zeros((count,), jnp.int32).at[ranking[jnp.where(places < fixed, places, passed)]].set(jnp.asarray(sizes, jnp.int32))

    sizes = jnp.where(number % 4 == 0, named(heavy_load, number // 4), named(common, number - number // 4 - 1))
    mixed = jax.random.permutation(jax.random.fold_in(own, 3), count)
    source_of, sink = mixed[0:count // 2 * 2:2], mixed[1:count // 2 * 2:2]
    margin = jnp.minimum(sizes[source_of] - 1, reach - sizes[sink]) // 2
    margin = jnp.where((source_of == ranking[0]) | (sink == ranking[0]) | (sizes[sink] == 0), 0, jnp.maximum(margin, 0))
    passed = jax.random.randint(jax.random.fold_in(own, 4), (count // 2,), 0, 1 << 20) % (margin + 1)
    sizes = sizes.at[source_of].add(-passed).at[sink].add(passed)
    labels = jnp.searchsorted(jnp.cumsum(sizes), jnp.arange(rows * top), side="right").astype(jnp.int32)
    table = labels.reshape(top, rows).T
    table = table[jax.random.permutation(jax.random.fold_in(own, 1), rows)]
    turn = jax.random.randint(jax.random.fold_in(own, 2), (rows, 1), 0, top)
    return jnp.take_along_axis(table, (jnp.arange(top)[None, :] + turn) % top, axis=1)


def load_shares(count, total, most, lean, full):
    loads = [(1 << 20) // math.isqrt(standing ** lean) + 1 for standing in range(1, count + 1)]
    largest = most if full else min(most, max(-(-total // count), total * loads[0] // sum(loads)))
    least = 1 if total - largest >= count - 1 else 0
    given, rest = [largest] + [least] * (count - 1), total - largest - least * (count - 1)
    while rest > 0:
        candidates = [i for i in range(1, count) if given[i] < largest] or [i for i in range(1, count) if given[i] < most]
        pool, budget = sum([loads[i] for i in candidates]), rest
        for i in candidates:
            extra = min(most - given[i], max(1, budget * loads[i] // pool), rest)
            given[i] = given[i] + extra
            rest = rest - extra
    return np.array(given)


def bell_draw(own_key, extent, spread, bound, cuts=(), kind=jnp.bfloat16):
    level = steps_of(own_key, extent, cuts, -0.22, 0.18) if cuts else 1.0
    drawn = jax.random.normal(own_key, extent, jnp.float32) * spread * level
    return jnp.minimum(jnp.maximum(drawn, -bound), bound).astype(kind)


def setup_inputs(seed: int = 0) -> dict:
    splits = jax.random.split(jax.random.key(seed), 6)
    stream = draw_stream(jax.random.fold_in(splits[5], 71), 0)
    routes_keys = jax.random.split(jax.random.fold_in(splits[1], 1), MB * SEQ // TOKM)
    routes_turns = jax.random.permutation(jax.random.fold_in(splits[1], 3), MB * SEQ // TOKM)
    routes = jax.vmap(lambda own, number: assign_block(jax.random.fold_in(splits[1], 2), own, number, TOKM, N_TOWER, 1, TOKM // 2, 2))(routes_keys, routes_turns).reshape((MB, SEQ, 1))
    tower_gain = jnp.clip(1.0 + 0.18 * jax.random.normal(splits[2], (N_SECTION, N_TOWER, D), jnp.float32), 0.1, 1.9)
    qkv_weight = draw_qkv_weight(jax.random.fold_in(splits[5], 71), 0)
    out_weight = bell_draw(splits[4], (N_SECTION, N_TOWER, HEADS, HD, D), (HEADS * HD) ** -0.5, 0.25, ((0, 2), (1, 4), (4, 4)))
    return dict(stream=stream, routes=routes, tower_gain=tower_gain, qkv_weight=qkv_weight, out_weight=out_weight)


NORM_EPSILON = 1e-05
MASKED = -1e+30

def tower_rows(row_towers, tower_at, capacity):
    outside = (row_towers != tower_at).astype(jnp.int32)
    ordered = jnp.argsort(outside, stable=True)[:capacity].astype(jnp.int32)
    return (ordered, row_towers[ordered] == tower_at)

def one_section(layer_input, row_towers, gain_rows, qkv_rows, out_rows):
    capacity = N_TOWER * (TOKM // 2)
    seq_len = layer_input.shape[0]
    squares = lax.optimization_barrier(jnp.sum(jnp.square(layer_input.astype(jnp.float32)), axis=1))
    inverse = lax.rsqrt(squares / D + NORM_EPSILON)
    mixed = jnp.zeros((seq_len, HEADS * 3 * HD), jnp.float32)
    for tower_at in range(N_TOWER):
        ordered, member = tower_rows(row_towers, tower_at, capacity)
        picked = layer_input[ordered]
        scaled = (picked.astype(jnp.float32) * gain_rows[tower_at]).astype(jnp.bfloat16)
        made = jnp.dot(scaled, qkv_rows[tower_at].reshape(D, HEADS * 3 * HD), preferred_element_type=jnp.float32)
        made = made * inverse[ordered][:, None]
        mixed = mixed.at[ordered].add(jnp.where(member[:, None], made, 0.0))
    triple = lax.optimization_barrier(mixed.reshape(seq_len, HEADS, 3, HD).astype(jnp.bfloat16)).astype(jnp.float32)
    queries = triple[:, :, 0]
    key_rows = triple[:, :, 1]
    values = triple[:, :, 2]
    scores = jnp.einsum('qhd,khd->hqk', queries, key_rows) * HD ** (-0.5)
    places = jnp.arange(seq_len, dtype=jnp.int32)
    visible = (places[None, :] <= places[:, None])[None]
    scores = jnp.where(visible, scores, MASKED)
    highest = lax.optimization_barrier(jnp.max(scores, axis=2, keepdims=True))
    expo = jnp.where(visible, jnp.exp(scores - highest), 0.0)
    weights = lax.optimization_barrier(expo.astype(jnp.bfloat16)).astype(jnp.float32)
    summed = jnp.einsum('hqk,khd->qhd', weights, values)
    denominator = lax.optimization_barrier(jnp.sum(expo, axis=2)).T
    attended = (summed / denominator[:, :, None]).astype(jnp.bfloat16).reshape(seq_len, HEADS * HD)
    projected = jnp.zeros((seq_len, D), jnp.float32)
    for tower_at in range(N_TOWER):
        ordered, member = tower_rows(row_towers, tower_at, capacity)
        made = jnp.dot(attended[ordered], out_rows[tower_at].reshape(HEADS * HD, D), preferred_element_type=jnp.float32)
        projected = projected.at[ordered].add(jnp.where(member[:, None], made, 0.0))
    return (layer_input.astype(jnp.float32) + projected).astype(jnp.bfloat16)

def reference(stream, routes, tower_gain, qkv_weight, out_weight):
    per_section = [[] for section_at in range(N_SECTION)]
    for micro_at in range(MB):
        current = stream[micro_at]
        row_towers = routes[micro_at, :, 0].astype(jnp.int32)
        for section_at in range(N_SECTION):
            current = one_section(current, row_towers, tower_gain[section_at], qkv_weight[section_at], out_weight[section_at])
            per_section[section_at].append(current)
    return jnp.stack([jnp.stack(group, axis=0) for group in per_section], axis=0)
```

```python
import functools

import jax
import jax.numpy as jnp
from jax import lax
from jax.experimental import pallas as pl
from jax.experimental.pallas import tpu as pltpu
from jax.sharding import PartitionSpec as P

NORM_EPSILON = 1e-05
MASKED = -1e30
MESH = pl.DeviceIdType.MESH


def unslot(spread, slots):
    return lax.dot_general(
        spread, slots, (((0,), (0,)), ((), ())), preferred_element_type=jnp.float32
    )


def kernel(
    sections, dps, towers,
    stream, routes, gain, qkv_hbm, out_hbm, out,
    w_in, w_out, routes_of, spread_of, rows_in, shares, outbound, inbound,
    queries, kv_out, kv_all, heads, updated, returned,
    w_sem, r_send, r_recv, z_send, z_recv, x_send, x_recv, kv_send, kv_recv,
    a_send, a_recv, b_send, b_recv, s_send, s_recv,
):
    micros, rows, width = stream.shape
    slots = rows // 2
    routed = towers * slots
    head = qkv_hbm.shape[2]
    section_at = lax.axis_index("section")
    dp_at = lax.axis_index("dp")
    tower_at = lax.axis_index("tower")
    next_section = lax.rem(section_at + 1, sections)
    prev_section = lax.rem(section_at + sections - 1, sections)

    def ahead(me, k, n):
        return lax.rem(me + k, n)

    weight_copies = [
        pltpu.make_async_copy(
            qkv_hbm.at[j], w_in.at[:, pl.ds(j * head, head)], w_sem.at[j]
        )
        for j in range(3)
    ]
    weight_copies.append(pltpu.make_async_copy(out_hbm, w_out, w_sem.at[3]))
    for copy in weight_copies:
        copy.start()

    barrier = pltpu.get_barrier_semaphore()
    for k in range(1, dps):
        pl.semaphore_signal(
            barrier, inc=1, device_id={"dp": ahead(dp_at, k, dps)}, device_id_type=MESH
        )
    for k in range(1, towers):
        pl.semaphore_signal(
            barrier, inc=1, device_id={"tower": ahead(tower_at, k, towers)}, device_id_type=MESH
        )

    @pl.when(section_at > 0)
    def _():
        pl.semaphore_signal(
            barrier, inc=1, device_id={"section": prev_section}, device_id_type=MESH
        )

    for m in range(micros):
        routes_of[tower_at, m : m + 1, 0:rows] = routes[m]

    @pl.when(section_at < sections - 1)
    def _():
        pl.semaphore_wait(barrier, dps + towers - 1)

    @pl.when(section_at == sections - 1)
    def _():
        pl.semaphore_wait(barrier, dps + towers - 2)

    started = []

    def send(src, dst, send_sem, recv_sem, device_id):
        copy = pltpu.make_async_remote_copy(
            src_ref=src, dst_ref=dst, send_sem=send_sem, recv_sem=recv_sem,
            device_id=device_id, device_id_type=MESH,
        )
        copy.start()
        started.append(copy)
        return copy

    route_copies = [
        send(
            routes_of.at[tower_at], routes_of.at[tower_at], r_send.at[k], r_recv.at[k],
            {"tower": ahead(tower_at, k, towers)},
        )
        for k in range(1, towers)
    ]

    lane = lax.broadcasted_iota(jnp.int32, (rows, rows), 1)
    sublane = lax.broadcasted_iota(jnp.int32, (rows, rows), 0)
    earlier = (sublane < lane).astype(jnp.bfloat16)
    tower_iota = lax.broadcasted_iota(jnp.int32, (16, rows), 0)
    slot_iota = lax.broadcasted_iota(jnp.int32, (slots, rows), 0).astype(jnp.float32)

    def make_spread(m, block):
        named = routes_of[block, m : m + 1, 0:rows]
        member = (jnp.broadcast_to(named, (16, rows)) == tower_iota).astype(jnp.float32)
        counted = jnp.dot(
            member.astype(jnp.bfloat16), earlier, preferred_element_type=jnp.float32
        )
        place = jnp.where(member > 0.0, counted, -1.0)
        for t in range(towers):
            hit = jnp.broadcast_to(place[t : t + 1], (slots, rows)) == slot_iota
            spread_of[m, block, t] = hit.astype(jnp.float32).astype(jnp.bfloat16)

    relays = [
        pltpu.make_async_remote_copy(
            src_ref=out.at[0, m], dst_ref=rows_in.at[m], send_sem=s_send.at[m],
            recv_sem=s_recv.at[m], device_id={"section": next_section}, device_id_type=MESH,
        )
        for m in range(micros)
    ]
    z_copies, x_copies, kv_copies, a_copies, b_copies = {}, {}, {}, {}, {}

    def enter(m):
        @pl.when(section_at == 0)
        def _():
            rows_in[m] = stream[m]

        @pl.when(section_at > 0)
        def _():
            relays[m].wait_recv()

        for k in range(1, dps):
            z_copies[m, k] = send(
                rows_in.at[m], shares.at[m, k], z_send.at[m, k], z_recv.at[m, k],
                {"dp": ahead(dp_at, k, dps)},
            )

    def route(m, k):
        if k == 0:
            share = rows_in[m]
        else:
            z_copies[m, k].wait_recv()
            share = shares[m, k]
        spread = spread_of[m, tower_at].reshape(routed, rows)
        picked = jnp.dot(spread, share, preferred_element_type=jnp.float32)
        outbound[m, k] = picked.astype(jnp.bfloat16).reshape(towers, slots, width)
        for j in range(1, towers):
            peer = ahead(tower_at, j, towers)
            x_copies[m, k, j] = send(
                outbound.at[m, k, peer], inbound.at[m, k, tower_at],
                x_send.at[m, k, j], x_recv.at[m, k, j], {"tower": peer},
            )
        inbound[m, k, tower_at] = outbound[m, k, tower_at]

    def project_in(m):
        total = jnp.zeros((routed, 3 * head), jnp.float32)
        squares = jnp.zeros((routed, 1), jnp.float32)
        for k in range(dps):
            for j in range(1, towers):
                x_copies[m, k, j].wait_recv()
            owner = lax.rem(dp_at + dps - k, dps)
            at = pl.ds(pl.multiple_of(owner * width, width), width)
            value = inbound[m, k].reshape(routed, width).astype(jnp.float32)
            squares = squares + jnp.sum(value * value, axis=1, keepdims=True)
            scaled = (value * gain[:, at]).astype(jnp.bfloat16)
            total = total + jnp.dot(scaled, w_in[at, :], preferred_element_type=jnp.float32)
        mixed = total * lax.rsqrt(squares / (width * dps) + NORM_EPSILON)
        queries[m] = mixed[:, :head].astype(jnp.bfloat16)
        kv_out[m] = mixed[:, head:].astype(jnp.bfloat16).reshape(towers, slots, 2 * head)
        for j in range(1, towers):
            kv_copies[m, j] = send(
                kv_out.at[m], kv_all.at[m, :, tower_at], kv_send.at[m, j], kv_recv.at[m, j],
                {"tower": ahead(tower_at, j, towers)},
            )
        for block in range(towers):
            kv_all[m, block, tower_at] = kv_out[m, block]

    def attend(m):
        place_iota = lax.broadcasted_iota(jnp.int32, (slots, rows), 1).astype(jnp.float32)
        anchors = jnp.concatenate(
            [
                jnp.sum(
                    spread_of[m, block, tower_at].astype(jnp.float32)
                    * (place_iota + float(block * rows)),
                    axis=1, keepdims=True,
                )
                for block in range(towers)
            ],
            axis=0,
        )
        for j in range(1, towers):
            kv_copies[m, j].wait_recv()
        kv = jnp.concatenate(
            [
                unslot(
                    spread_of[m, block].reshape(routed, rows),
                    kv_all[m, block].reshape(routed, 2 * head),
                ).astype(jnp.bfloat16)
                for block in range(towers)
            ],
            axis=0,
        )
        scores = lax.dot_general(
            queries[m], kv[:, :head], (((1,), (1,)), ((), ())),
            preferred_element_type=jnp.float32,
        ) * (head ** -0.5)
        column = lax.broadcasted_iota(jnp.int32, scores.shape, 1).astype(jnp.float32)
        visible = column <= anchors
        scores = jnp.where(visible, scores, MASKED)
        highest = jnp.max(scores, axis=1, keepdims=True)
        weights = jnp.where(visible, jnp.exp(scores - highest), 0.0)
        denominator = jnp.sum(weights, axis=1, keepdims=True)
        summed = jnp.dot(
            weights.astype(jnp.bfloat16), kv[:, head:], preferred_element_type=jnp.float32
        )
        own = pl.ds(pl.multiple_of(dp_at * head, head), head)
        heads[m, :, own] = (summed / denominator).astype(jnp.bfloat16)
        for k in range(1, dps):
            a_copies[m, k] = send(
                heads.at[m, :, own], heads.at[m, :, own], a_send.at[m, k], a_recv.at[m, k],
                {"dp": ahead(dp_at, k, dps)},
            )

    def project_out(m):
        for k in range(1, dps):
            a_copies[m, k].wait_recv()
        made = jnp.dot(heads[m], w_out[...], preferred_element_type=jnp.float32)
        own = inbound[m, 0].reshape(routed, width).astype(jnp.float32)
        updated[m] = (own + made).astype(jnp.bfloat16).reshape(towers, slots, width)
        for j in range(1, towers):
            peer = ahead(tower_at, j, towers)
            b_copies[m, j] = send(
                updated.at[m, peer], returned.at[m, tower_at], b_send.at[m, j], b_recv.at[m, j],
                {"tower": peer},
            )
        returned[m, tower_at] = updated[m, tower_at]

    def leave(m):
        for j in range(1, towers):
            b_copies[m, j].wait_recv()
        spread = spread_of[m, tower_at].reshape(routed, rows)
        out[0, m] = unslot(spread, returned[m].reshape(routed, width)).astype(jnp.bfloat16)

        @pl.when(section_at < sections - 1)
        def _():
            relays[m].start()

    for m in range(micros):
        make_spread(m, tower_at)
    enter(0)
    for k in range(dps):
        route(0, k)
    for k in range(1, towers):
        route_copies[k - 1].wait_recv()
        for m in range(micros):
            make_spread(m, lax.rem(tower_at + towers - k, towers))
    for copy in weight_copies:
        copy.wait()

    later = [project_in, attend, project_out, leave]
    for m in range(micros):
        pending = list(range(dps)) if m + 1 < micros else []
        if pending:
            enter(m + 1)
            route(m + 1, pending.pop(0))
        for number, step in enumerate(later):
            step(m)
            left = len(later) - 1 - number
            if pending and left:
                for k in range(-(-len(pending) // left)):
                    route(m + 1, pending.pop(0))

    for copy in started:
        copy.wait_send()

    @pl.when(section_at < sections - 1)
    def _():
        for m in range(micros):
            relays[m].wait_send()


def shards(stream, routes, tower_gain, qkv_weight, out_weight):
    micros, rows, width = stream.shape
    sections = lax.axis_size("section")
    dps = lax.axis_size("dp")
    towers = lax.axis_size("tower")
    head = qkv_weight.shape[-1]
    model = tower_gain.shape[-1]
    slots = rows // 2
    routed = towers * slots
    bf16 = jnp.bfloat16
    dma = pltpu.SemaphoreType.DMA
    vmem = pl.BlockSpec(memory_space=pltpu.VMEM)
    hbm = pl.BlockSpec(memory_space=pl.ANY)
    return pl.pallas_call(
        functools.partial(kernel, sections, dps, towers),
        out_shape=jax.ShapeDtypeStruct((1, micros, rows, width), bf16),
        in_specs=[vmem, vmem, vmem, hbm, hbm],
        out_specs=vmem,
        scratch_shapes=[
            pltpu.VMEM((model, 3 * head), bf16),
            pltpu.VMEM((dps * head, width), bf16),
            pltpu.VMEM((towers, 8, 128), jnp.int32),
            pltpu.VMEM((micros, towers, towers, slots, rows), bf16),
            pltpu.VMEM((micros, rows, width), bf16),
            pltpu.VMEM((micros, dps, rows, width), bf16),
            pltpu.VMEM((micros, dps, towers, slots, width), bf16),
            pltpu.VMEM((micros, dps, towers, slots, width), bf16),
            pltpu.VMEM((micros, routed, head), bf16),
            pltpu.VMEM((micros, towers, slots, 2 * head), bf16),
            pltpu.VMEM((micros, towers, towers, slots, 2 * head), bf16),
            pltpu.VMEM((micros, routed, dps * head), bf16),
            pltpu.VMEM((micros, towers, slots, width), bf16),
            pltpu.VMEM((micros, towers, slots, width), bf16),
            dma((4,)),
            dma((towers,)), dma((towers,)),
            dma((micros, dps)), dma((micros, dps)),
            dma((micros, dps, towers)), dma((micros, dps, towers)),
            dma((micros, towers)), dma((micros, towers)),
            dma((micros, dps)), dma((micros, dps)),
            dma((micros, towers)), dma((micros, towers)),
            dma((micros,)), dma((micros,)),
        ],
        compiler_params=pltpu.CompilerParams(
            collective_id=0, has_side_effects=True, vmem_limit_bytes=48 * 1024 * 1024
        ),
        name="relay",
    )(
        stream,
        jnp.transpose(routes, (0, 2, 1)),
        tower_gain.reshape(1, model),
        jnp.transpose(qkv_weight.reshape(model, 3, head), (1, 0, 2)),
        out_weight.reshape(dps * head, width),
    )


def solution(mesh):
    placed = (
        P(None, "tower", "dp"),
        P(None, "tower", None),
        P("section", "tower", None),
        P("section", "tower", None, "dp", None, None),
        P("section", "tower", None, None, "dp"),
    )
    return jax.shard_map(
        shards,
        mesh=mesh,
        in_specs=placed,
        out_specs=P("section", None, "tower", "dp"),
        check_vma=False,
    )
```

```python
import functools

import jax
import jax.numpy as jnp
from jax import lax
from jax.experimental import pallas as pl
from jax.experimental.pallas import tpu as pltpu
from jax.sharding import PartitionSpec as P

NORM_EPSILON = 1e-05
MASKED = -1e30
MESH = pl.DeviceIdType.MESH


def unslot(spread, slots):
    return lax.dot_general(
        spread, slots, (((0,), (0,)), ((), ())), preferred_element_type=jnp.float32
    )


def kernel(
    sections, dps, towers,
    stream, routes, gain_hbm, qkv_hbm, out_hbm, out,
    w_in, w_out, gain, routes_in, routes_of, spread_of, shares, outbound, inbound,
    total, squares, queries, kv_out, kv_all, heads, updated, returned,
    w_sem, r_send, r_recv, z_send, z_recv, x_send, x_recv, kv_send, kv_recv,
    a_send, a_recv, b_send, b_recv, s_send, s_recv,
):
    micros, rows, width = stream.shape
    slots = rows // 2
    routed = towers * slots
    head = qkv_hbm.shape[2]
    part = shares.shape[3]
    parts = width // part
    section_at = lax.axis_index("section")
    dp_at = lax.axis_index("dp")
    tower_at = lax.axis_index("tower")
    next_section = lax.rem(section_at + 1, sections)
    prev_section = lax.rem(section_at + sections - 1, sections)

    def ahead(me, k, n):
        return lax.rem(me + k, n)

    weight_copies = [
        pltpu.make_async_copy(
            qkv_hbm.at[j], w_in.at[:, pl.ds(j * head, head)], w_sem.at[j]
        )
        for j in range(3)
    ]
    weight_copies.append(pltpu.make_async_copy(out_hbm, w_out, w_sem.at[3]))
    weight_copies.append(pltpu.make_async_copy(gain_hbm, gain, w_sem.at[4]))
    routes_copy = pltpu.make_async_copy(routes, routes_in, w_sem.at[5])
    routes_copy.start()
    stream_copies = [
        pltpu.make_async_copy(
            stream.at[u // parts, :, pl.ds(u % parts * part, part)],
            shares.at[u, dp_at], w_sem.at[6 + u],
        )
        for u in range(micros * parts)
    ]

    @pl.when(section_at == 0)
    def _():
        for copy in stream_copies:
            copy.start()

    for copy in weight_copies:
        copy.start()

    barrier = pltpu.get_barrier_semaphore()
    for k in range(1, dps):
        pl.semaphore_signal(
            barrier, inc=1, device_id={"dp": ahead(dp_at, k, dps)}, device_id_type=MESH
        )
    for k in range(1, towers):
        pl.semaphore_signal(
            barrier, inc=1, device_id={"tower": ahead(tower_at, k, towers)}, device_id_type=MESH
        )

    @pl.when(section_at > 0)
    def _():
        pl.semaphore_signal(
            barrier, inc=1, device_id={"section": prev_section}, device_id_type=MESH
        )

    routes_copy.wait()
    for m in range(micros):
        routes_of[tower_at, m : m + 1, 0:rows] = routes_in[m]

    @pl.when(section_at < sections - 1)
    def _():
        pl.semaphore_wait(barrier, dps + towers - 1)

    @pl.when(section_at == sections - 1)
    def _():
        pl.semaphore_wait(barrier, dps + towers - 2)

    started = []

    def send(src, dst, send_sem, recv_sem, device_id):
        copy = pltpu.make_async_remote_copy(
            src_ref=src, dst_ref=dst, send_sem=send_sem, recv_sem=recv_sem,
            device_id=device_id, device_id_type=MESH,
        )
        copy.start()
        started.append(copy)
        return copy

    route_copies = [
        send(
            routes_of.at[tower_at], routes_of.at[tower_at], r_send.at[k], r_recv.at[k],
            {"tower": ahead(tower_at, k, towers)},
        )
        for k in range(1, towers)
    ]

    lane = lax.broadcasted_iota(jnp.int32, (rows, rows), 1)
    sublane = lax.broadcasted_iota(jnp.int32, (rows, rows), 0)
    earlier = (sublane < lane).astype(jnp.bfloat16)
    tower_iota = lax.broadcasted_iota(jnp.int32, (16, rows), 0)
    slot_iota = lax.broadcasted_iota(jnp.int32, (slots, rows), 0).astype(jnp.float32)

    def make_spread(m, block):
        named = routes_of[block, m : m + 1, 0:rows]
        member = (jnp.broadcast_to(named, (16, rows)) == tower_iota).astype(jnp.float32)
        counted = jnp.dot(
            member.astype(jnp.bfloat16), earlier, preferred_element_type=jnp.float32
        )
        place = jnp.where(member > 0.0, counted, -1.0)
        for t in range(towers):
            hit = jnp.broadcast_to(place[t : t + 1], (slots, rows)) == slot_iota
            spread_of[m, block, t] = hit.astype(jnp.float32).astype(jnp.bfloat16)

    relays = [
        pltpu.make_async_remote_copy(
            src_ref=out.at[0, u // parts, :, pl.ds(u % parts * part, part)],
            dst_ref=shares.at[u, dp_at], send_sem=s_send.at[u],
            recv_sem=s_recv.at[u], device_id={"section": next_section}, device_id_type=MESH,
        )
        for u in range(micros * parts)
    ]
    kv_copies, a_copies, b_copies = {}, {}, {}

    def pass_on(u, owner, way):
        return pltpu.make_async_remote_copy(
            src_ref=shares.at[u, owner], dst_ref=shares.at[u, owner],
            send_sem=z_send.at[u, way, owner], recv_sem=z_recv.at[u, owner],
            device_id={"dp": lax.rem(dp_at + (1 if way else dps - 1), dps)}, device_id_type=MESH,
        )

    def tower_copy(u, owner, j):
        peer = ahead(tower_at, j, towers)
        return pltpu.make_async_remote_copy(
            src_ref=outbound.at[u, owner, peer], dst_ref=inbound.at[u, owner, tower_at],
            send_sem=x_send.at[u, owner, j], recv_sem=x_recv.at[u, owner, j],
            device_id={"tower": peer}, device_id_type=MESH,
        )

    def forward(u, owner, way):
        @pl.when(dp_at < dps - 1 if way else dp_at > 0)
        def _():
            pass_on(u, owner, way).start()

    def begin(m, ready):
        for u in range(m * parts, (m + 1) * parts):
            ready(u)
            if dps > 1:
                forward(u, dp_at, 0)
                forward(u, dp_at, 1)
            route(u, dp_at)

    def enter_first(m):
        @pl.when(section_at == 0)
        def _():
            begin(m, lambda u: stream_copies[u].wait())

    def enter_later(m):
        @pl.when(section_at > 0)
        def _():
            begin(m, lambda u: relays[u].wait_recv())

    def route(m, owner):
        spread = spread_of[m // parts, tower_at].reshape(routed, rows)
        picked = jnp.dot(spread, shares[m, owner], preferred_element_type=jnp.float32)
        outbound[m, owner] = picked.astype(jnp.bfloat16).reshape(towers, slots, part)
        for j in range(1, towers):
            tower_copy(m, owner, j).start()
        inbound[m, owner, tower_at] = outbound[m, owner, tower_at]

    def both_sides(k, act):
        @pl.when(dp_at >= k)
        def _():
            act(dp_at - k, 1)

        @pl.when(dp_at < dps - k)
        def _():
            act(dp_at + k, 0)

    def hop(m, k):
        for u in range(m * parts, (m + 1) * parts):
            def act(owner, way):
                pass_on(u, owner, way).wait_recv()
                forward(u, owner, way)
                route(u, owner)

            both_sides(k, act)

    def gather_in(m, owner, first):
        at = pl.ds(pl.multiple_of(owner * width + m % parts * part, part), part)
        for j in range(1, towers):
            tower_copy(m, owner, j).wait_recv()
        value = inbound[m, owner].reshape(routed, part).astype(jnp.float32)
        square = jnp.sum(value * value, axis=1, keepdims=True)
        scaled = (value * gain[:, at]).astype(jnp.bfloat16)
        made = jnp.dot(scaled, w_in[at, :], preferred_element_type=jnp.float32)
        if first:
            squares[...] = jnp.broadcast_to(square, squares.shape)
            total[...] = made
        else:
            squares[...] += jnp.broadcast_to(square, squares.shape)
            total[...] += made

    def collect(m, k):
        for u in range(m * parts, (m + 1) * parts):
            if k == 0:
                gather_in(u, dp_at, u % parts == 0)
            else:
                both_sides(k, lambda owner, way: gather_in(u, owner, False))

    def project_in(m):
        inverse = lax.rsqrt(squares[:, 0:1] / (width * dps) + NORM_EPSILON)
        mixed = total[...] * inverse
        queries[m] = mixed[:, :head].astype(jnp.bfloat16)
        kv_out[m] = mixed[:, head:].astype(jnp.bfloat16).reshape(towers, slots, 2 * head)
        for j in range(1, towers):
            kv_copies[m, j] = send(
                kv_out.at[m], kv_all.at[m, :, tower_at], kv_send.at[m, j], kv_recv.at[m, j],
                {"tower": ahead(tower_at, j, towers)},
            )
        for block in range(towers):
            kv_all[m, block, tower_at] = kv_out[m, block]

    def attend(m):
        place_iota = lax.broadcasted_iota(jnp.int32, (slots, rows), 1).astype(jnp.float32)
        anchors = jnp.concatenate(
            [
                jnp.sum(
                    spread_of[m, block, tower_at].astype(jnp.float32)
                    * (place_iota + float(block * rows)),
                    axis=1, keepdims=True,
                )
                for block in range(towers)
            ],
            axis=0,
        )
        for j in range(1, towers):
            kv_copies[m, j].wait_recv()
        kv = jnp.concatenate(
            [
                unslot(
                    spread_of[m, block].reshape(routed, rows),
                    kv_all[m, block].reshape(routed, 2 * head),
                ).astype(jnp.bfloat16)
                for block in range(towers)
            ],
            axis=0,
        )
        scores = lax.dot_general(
            queries[m], kv[:, :head], (((1,), (1,)), ((), ())),
            preferred_element_type=jnp.float32,
        ) * (head ** -0.5)
        column = lax.broadcasted_iota(jnp.int32, scores.shape, 1).astype(jnp.float32)
        visible = column <= anchors
        scores = jnp.where(visible, scores, MASKED)
        highest = jnp.max(scores, axis=1, keepdims=True)
        weights = jnp.where(visible, jnp.exp(scores - highest), 0.0)
        denominator = jnp.sum(weights, axis=1, keepdims=True)
        summed = jnp.dot(
            weights.astype(jnp.bfloat16), kv[:, head:], preferred_element_type=jnp.float32
        )
        own = pl.ds(pl.multiple_of(dp_at * head, head), head)
        heads[m, :, own] = (summed / denominator).astype(jnp.bfloat16)
        for k in range(1, dps):
            a_copies[m, k] = send(
                heads.at[m, :, own], heads.at[m, :, own], a_send.at[m, k], a_recv.at[m, k],
                {"dp": ahead(dp_at, k, dps)},
            )

    def project_out(m):
        for k in range(1, dps):
            a_copies[m, k].wait_recv()
        for c in range(parts):
            u = m * parts + c
            made = jnp.dot(
                heads[m], w_out[:, c * part : (c + 1) * part], preferred_element_type=jnp.float32
            )
            own = inbound[u, dp_at].reshape(routed, part).astype(jnp.float32)
            updated[u] = (own + made).astype(jnp.bfloat16).reshape(towers, slots, part)
            for j in range(1, towers):
                peer = ahead(tower_at, j, towers)
                b_copies[u, j] = send(
                    updated.at[u, peer], returned.at[u, tower_at],
                    b_send.at[u, j], b_recv.at[u, j], {"tower": peer},
                )
            returned[u, tower_at] = updated[u, tower_at]

    def leave(m):
        spread = spread_of[m, tower_at].reshape(routed, rows)
        for c in range(parts):
            u = m * parts + c
            for j in range(1, towers):
                b_copies[u, j].wait_recv()
            moved = unslot(spread, returned[u].reshape(routed, part))
            out[0, m, :, c * part : (c + 1) * part] = moved.astype(jnp.bfloat16)

            @pl.when(section_at < sections - 1)
            def _():
                relays[u].start()

    for m in range(micros):
        make_spread(m, tower_at)
    enter_first(0)
    enter_later(0)
    for k in range(1, dps):
        hop(0, k)
        if k == 1:
            for copy in weight_copies:
                copy.wait()
            for j in range(1, towers):
                route_copies[j - 1].wait_recv()
                for n in range(micros):
                    make_spread(n, lax.rem(tower_at + towers - j, towers))
        if k == max(1, dps - 2) and micros > 1:
            enter_first(1)
        collect(0, k - 1)
    for m in range(micros):
        collect(m, dps - 1)
        project_in(m)
        following = m + 1 < micros
        if following:
            enter_later(m + 1)
            for k in range(1, dps - 1):
                hop(m + 1, k)
        attend(m)
        if following:
            hop(m + 1, dps - 1)
        project_out(m)
        if following:
            collect(m + 1, 0)
        leave(m)
        if following:
            if m + 2 < micros:
                enter_first(m + 2)
            for k in range(1, dps - 1):
                collect(m + 1, k)

    for copy in started:
        copy.wait_send()
    for u in range(micros * parts):
        for owner in range(dps):
            for j in range(1, towers):
                tower_copy(u, owner, j).wait_send()

            @pl.when((dp_at >= owner) & (dp_at < dps - 1))
            def _():
                pass_on(u, owner, 1).wait_send()

            @pl.when((dp_at <= owner) & (dp_at > 0))
            def _():
                pass_on(u, owner, 0).wait_send()

    @pl.when(section_at < sections - 1)
    def _():
        for u in range(micros * parts):
            relays[u].wait_send()


def shards(stream, routes, tower_gain, qkv_weight, out_weight):
    micros, rows, width = stream.shape
    sections = lax.axis_size("section")
    dps = lax.axis_size("dp")
    towers = lax.axis_size("tower")
    head = qkv_weight.shape[-1]
    model = tower_gain.shape[-1]
    slots = rows // 2
    routed = towers * slots
    parts = 2
    units = micros * parts
    part = width // parts
    bf16 = jnp.bfloat16
    dma = pltpu.SemaphoreType.DMA
    vmem = pl.BlockSpec(memory_space=pltpu.VMEM)
    hbm = pl.BlockSpec(memory_space=pl.ANY)
    return pl.pallas_call(
        functools.partial(kernel, sections, dps, towers),
        out_shape=jax.ShapeDtypeStruct((1, micros, rows, width), bf16),
        in_specs=[hbm] * 5,
        out_specs=vmem,
        scratch_shapes=[
            pltpu.VMEM((model, 3 * head), bf16),
            pltpu.VMEM((dps * head, width), bf16),
            pltpu.VMEM((1, model), jnp.float32),
            pltpu.VMEM((micros, 1, rows), jnp.int32),
            pltpu.VMEM((towers, 8, 128), jnp.int32),
            pltpu.VMEM((micros, towers, towers, slots, rows), bf16),
            pltpu.VMEM((units, dps, rows, part), bf16),
            pltpu.VMEM((units, dps, towers, slots, part), bf16),
            pltpu.VMEM((units, dps, towers, slots, part), bf16),
            pltpu.VMEM((routed, 3 * head), jnp.float32),
            pltpu.VMEM((routed, 128), jnp.float32),
            pltpu.VMEM((micros, routed, head), bf16),
            pltpu.VMEM((micros, towers, slots, 2 * head), bf16),
            pltpu.VMEM((micros, towers, towers, slots, 2 * head), bf16),
            pltpu.VMEM((micros, routed, dps * head), bf16),
            pltpu.VMEM((units, towers, slots, part), bf16),
            pltpu.VMEM((units, towers, slots, part), bf16),
            dma((6 + units,)),
            dma((towers,)), dma((towers,)),
            dma((units, 2, dps)), dma((units, dps)),
            dma((units, dps, towers)), dma((units, dps, towers)),
            dma((micros, towers)), dma((micros, towers)),
            dma((micros, dps)), dma((micros, dps)),
            dma((units, towers)), dma((units, towers)),
            dma((units,)), dma((units,)),
        ],
        compiler_params=pltpu.CompilerParams(
            collective_id=0, has_side_effects=True, vmem_limit_bytes=60 * 1024 * 1024
        ),
        name="relay",
    )(
        stream,
        jnp.transpose(routes, (0, 2, 1)),
        tower_gain.reshape(1, model),
        jnp.transpose(qkv_weight.reshape(model, 3, head), (1, 0, 2)),
        out_weight.reshape(dps * head, width),
    )


def solution(mesh):
    placed = (
        P(None, "tower", "dp"),
        P(None, "tower", None),
        P("section", "tower", None),
        P("section", "tower", None, "dp", None, None),
        P("section", "tower", None, None, "dp"),
    )
    return jax.shard_map(
        shards,
        mesh=mesh,
        in_specs=placed,
        out_specs=P("section", None, "tower", "dp"),
        check_vma=False,
    )
```

```python
import functools

import jax
import jax.numpy as jnp
from jax import lax
from jax.experimental import pallas as pl
from jax.experimental.pallas import tpu as pltpu
from jax.sharding import PartitionSpec as P

NORM_EPSILON = 1e-05
MASKED = -1e30
MESH = pl.DeviceIdType.MESH


def unslot(spread, slots):
    return lax.dot_general(
        spread, slots, (((0,), (0,)), ((), ())), preferred_element_type=jnp.float32
    )


def kernel(
    sections, dps, towers,
    stream, routes, gain_hbm, qkv_hbm, out_hbm, out,
    w_in, w_out, gain, routes_in, routes_of, spread_of, shares, outbound, inbound,
    total, squares, queries, kv_out, kv_all, heads, updated, returned,
    w_sem, r_send, r_recv, z_send, z_recv, x_send, x_recv, kv_send, kv_recv,
    a_send, a_recv, b_send, b_recv, s_send, s_recv,
):
    micros, rows, width = stream.shape
    slots = rows // 2
    routed = towers * slots
    head = qkv_hbm.shape[2]
    part = shares.shape[3]
    parts = width // part
    section_at = lax.axis_index("section")
    dp_at = lax.axis_index("dp")
    tower_at = lax.axis_index("tower")
    next_section = lax.rem(section_at + 1, sections)
    prev_section = lax.rem(section_at + sections - 1, sections)

    def ahead(me, k, n):
        return lax.rem(me + k, n)

    weight_copies = [
        pltpu.make_async_copy(
            qkv_hbm.at[j], w_in.at[:, pl.ds(j * head, head)], w_sem.at[j]
        )
        for j in range(3)
    ]
    weight_copies.append(pltpu.make_async_copy(out_hbm, w_out, w_sem.at[3]))
    weight_copies.append(pltpu.make_async_copy(gain_hbm, gain, w_sem.at[4]))
    routes_copy = pltpu.make_async_copy(routes, routes_in, w_sem.at[5])
    routes_copy.start()
    stream_copies = [
        pltpu.make_async_copy(
            stream.at[u // parts, :, pl.ds(u % parts * part, part)],
            shares.at[u, dp_at], w_sem.at[6 + u],
        )
        for u in range(micros * parts)
    ]

    @pl.when(section_at == 0)
    def _():
        for copy in stream_copies:
            copy.start()

    for copy in weight_copies:
        copy.start()

    barrier = pltpu.get_barrier_semaphore()
    for k in range(1, dps):
        pl.semaphore_signal(
            barrier, inc=1, device_id={"dp": ahead(dp_at, k, dps)}, device_id_type=MESH
        )
    for k in range(1, towers):
        pl.semaphore_signal(
            barrier, inc=1, device_id={"tower": ahead(tower_at, k, towers)}, device_id_type=MESH
        )

    @pl.when(section_at > 0)
    def _():
        pl.semaphore_signal(
            barrier, inc=1, device_id={"section": prev_section}, device_id_type=MESH
        )

    routes_copy.wait()
    for m in range(micros):
        routes_of[tower_at, m : m + 1, 0:rows] = routes_in[m]

    @pl.when(section_at < sections - 1)
    def _():
        pl.semaphore_wait(barrier, dps + towers - 1)

    @pl.when(section_at == sections - 1)
    def _():
        pl.semaphore_wait(barrier, dps + towers - 2)

    started = []

    def send(src, dst, send_sem, recv_sem, device_id):
        copy = pltpu.make_async_remote_copy(
            src_ref=src, dst_ref=dst, send_sem=send_sem, recv_sem=recv_sem,
            device_id=device_id, device_id_type=MESH,
        )
        copy.start()
        started.append(copy)
        return copy

    route_copies = [
        send(
            routes_of.at[tower_at], routes_of.at[tower_at], r_send.at[k], r_recv.at[k],
            {"tower": ahead(tower_at, k, towers)},
        )
        for k in range(1, towers)
    ]

    lane = lax.broadcasted_iota(jnp.int32, (rows, rows), 1)
    sublane = lax.broadcasted_iota(jnp.int32, (rows, rows), 0)
    earlier = (sublane < lane).astype(jnp.bfloat16)
    tower_iota = lax.broadcasted_iota(jnp.int32, (16, rows), 0)
    slot_iota = lax.broadcasted_iota(jnp.int32, (slots, rows), 0).astype(jnp.float32)

    def make_spread(m, block):
        named = routes_of[block, m : m + 1, 0:rows]
        member = (jnp.broadcast_to(named, (16, rows)) == tower_iota).astype(jnp.float32)
        counted = jnp.dot(
            member.astype(jnp.bfloat16), earlier, preferred_element_type=jnp.float32
        )
        place = jnp.where(member > 0.0, counted, -1.0)
        for t in range(towers):
            hit = jnp.broadcast_to(place[t : t + 1], (slots, rows)) == slot_iota
            spread_of[m, block, t] = hit.astype(jnp.float32).astype(jnp.bfloat16)

    relays = [
        pltpu.make_async_remote_copy(
            src_ref=out.at[0, u // parts, :, pl.ds(u % parts * part, part)],
            dst_ref=shares.at[u, dp_at], send_sem=s_send.at[u],
            recv_sem=s_recv.at[u], device_id={"section": next_section}, device_id_type=MESH,
        )
        for u in range(micros * parts)
    ]
    kv_copies, a_copies, b_copies = {}, {}, {}

    def pass_on(u, owner, way):
        return pltpu.make_async_remote_copy(
            src_ref=shares.at[u, owner], dst_ref=shares.at[u, owner],
            send_sem=z_send.at[u, way, owner], recv_sem=z_recv.at[u, owner],
            device_id={"dp": lax.rem(dp_at + (1 if way else dps - 1), dps)}, device_id_type=MESH,
        )

    def tower_copy(u, owner, j):
        peer = ahead(tower_at, j, towers)
        return pltpu.make_async_remote_copy(
            src_ref=outbound.at[u, owner, peer], dst_ref=inbound.at[u, owner, tower_at],
            send_sem=x_send.at[u, owner, j], recv_sem=x_recv.at[u, owner, j],
            device_id={"tower": peer}, device_id_type=MESH,
        )

    def forward(u, owner, way):
        @pl.when(dp_at < dps - 1 if way else dp_at > 0)
        def _():
            pass_on(u, owner, way).start()

    def begin(m, ready):
        for u in range(m * parts, (m + 1) * parts):
            ready(u)
            if dps > 1:
                forward(u, dp_at, 0)
                forward(u, dp_at, 1)
            route(u, dp_at)

    def enter_first(m):
        @pl.when(section_at == 0)
        def _():
            begin(m, lambda u: stream_copies[u].wait())

    def enter_later(m):
        @pl.when(section_at > 0)
        def _():
            begin(m, lambda u: relays[u].wait_recv())

    def route(m, owner):
        spread = spread_of[m // parts, tower_at].reshape(routed, rows)
        picked = jnp.dot(spread, shares[m, owner], preferred_element_type=jnp.float32)
        outbound[m, owner] = picked.astype(jnp.bfloat16).reshape(towers, slots, part)
        for j in range(1, towers):
            tower_copy(m, owner, j).start()
        inbound[m, owner, tower_at] = outbound[m, owner, tower_at]

    def both_sides(k, act):
        @pl.when(dp_at >= k)
        def _():
            act(dp_at - k, 1)

        @pl.when(dp_at < dps - k)
        def _():
            act(dp_at + k, 0)

    def hop(m, k):
        for u in range(m * parts, (m + 1) * parts):
            def act(owner, way):
                pass_on(u, owner, way).wait_recv()
                forward(u, owner, way)
                route(u, owner)

            both_sides(k, act)

    def gather_in(m, owner, first):
        at = pl.ds(pl.multiple_of(owner * width + m % parts * part, part), part)
        for j in range(1, towers):
            tower_copy(m, owner, j).wait_recv()
        value = inbound[m, owner].reshape(routed, part).astype(jnp.float32)
        square = jnp.sum(value * value, axis=1, keepdims=True)
        scaled = (value * gain[:, at]).astype(jnp.bfloat16)
        made = jnp.dot(scaled, w_in[at, :], preferred_element_type=jnp.float32)
        if first:
            squares[...] = jnp.broadcast_to(square, squares.shape)
            total[...] = made
        else:
            squares[...] += jnp.broadcast_to(square, squares.shape)
            total[...] += made

    def collect(m, k):
        for u in range(m * parts, (m + 1) * parts):
            if k == 0:
                gather_in(u, dp_at, u % parts == 0)
            else:
                both_sides(k, lambda owner, way: gather_in(u, owner, False))

    def project_in(m):
        inverse = lax.rsqrt(squares[:, 0:1] / (width * dps) + NORM_EPSILON)
        mixed = total[...] * inverse
        queries[m] = mixed[:, :head].astype(jnp.bfloat16)
        kv_out[m] = mixed[:, head:].astype(jnp.bfloat16).reshape(towers, slots, 2 * head)
        for j in range(1, towers):
            kv_copies[m, j] = send(
                kv_out.at[m], kv_all.at[m, :, tower_at], kv_send.at[m, j], kv_recv.at[m, j],
                {"tower": ahead(tower_at, j, towers)},
            )
        for block in range(towers):
            kv_all[m, block, tower_at] = kv_out[m, block]

    def attend(m):
        place_iota = lax.broadcasted_iota(jnp.int32, (slots, rows), 1).astype(jnp.float32)
        anchors = jnp.concatenate(
            [
                jnp.sum(
                    spread_of[m, block, tower_at].astype(jnp.float32)
                    * (place_iota + float(block * rows)),
                    axis=1, keepdims=True,
                )
                for block in range(towers)
            ],
            axis=0,
        )
        for j in range(1, towers):
            kv_copies[m, j].wait_recv()
        kv = jnp.concatenate(
            [
                unslot(
                    spread_of[m, block].reshape(routed, rows),
                    kv_all[m, block].reshape(routed, 2 * head),
                ).astype(jnp.bfloat16)
                for block in range(towers)
            ],
            axis=0,
        )
        scores = lax.dot_general(
            queries[m], kv[:, :head], (((1,), (1,)), ((), ())),
            preferred_element_type=jnp.float32,
        ) * (head ** -0.5)
        column = lax.broadcasted_iota(jnp.int32, scores.shape, 1).astype(jnp.float32)
        visible = column <= anchors
        scores = jnp.where(visible, scores, MASKED)
        highest = jnp.max(scores, axis=1, keepdims=True)
        weights = jnp.where(visible, jnp.exp(scores - highest), 0.0)
        denominator = jnp.sum(weights, axis=1, keepdims=True)
        summed = jnp.dot(
            weights.astype(jnp.bfloat16), kv[:, head:], preferred_element_type=jnp.float32
        )
        own = pl.ds(pl.multiple_of(dp_at * head, head), head)
        heads[m, :, own] = (summed / denominator).astype(jnp.bfloat16)
        for k in range(1, dps):
            a_copies[m, k] = send(
                heads.at[m, :, own], heads.at[m, :, own], a_send.at[m, k], a_recv.at[m, k],
                {"dp": ahead(dp_at, k, dps)},
            )

    def project_out(m):
        for k in range(1, dps):
            a_copies[m, k].wait_recv()
        for c in range(parts):
            u = m * parts + c
            made = jnp.dot(
                heads[m], w_out[:, c * part : (c + 1) * part], preferred_element_type=jnp.float32
            )
            own = inbound[u, dp_at].reshape(routed, part).astype(jnp.float32)
            updated[u] = (own + made).astype(jnp.bfloat16).reshape(towers, slots, part)
            for j in range(1, towers):
                peer = ahead(tower_at, j, towers)
                b_copies[u, j] = send(
                    updated.at[u, peer], returned.at[u, tower_at],
                    b_send.at[u, j], b_recv.at[u, j], {"tower": peer},
                )
            returned[u, tower_at] = updated[u, tower_at]

    def leave(m):
        spread = spread_of[m, tower_at].reshape(routed, rows)
        for c in range(parts):
            u = m * parts + c
            for j in range(1, towers):
                b_copies[u, j].wait_recv()
            moved = unslot(spread, returned[u].reshape(routed, part))
            out[0, m, :, c * part : (c + 1) * part] = moved.astype(jnp.bfloat16)

            @pl.when(section_at < sections - 1)
            def _():
                relays[u].start()

    for m in range(micros):
        make_spread(m, tower_at)
    enter_first(0)
    enter_later(0)
    for k in range(1, dps):
        hop(0, k)
        if k == 1:
            for copy in weight_copies:
                copy.wait()
            for j in range(1, towers):
                route_copies[j - 1].wait_recv()
                for n in range(micros):
                    make_spread(n, lax.rem(tower_at + towers - j, towers))
        if k == max(1, dps - 2) and micros > 1:
            enter_first(1)
        collect(0, k - 1)
    for m in range(micros):
        collect(m, dps - 1)
        project_in(m)
        following = m + 1 < micros
        if following:
            enter_later(m + 1)
        attend(m)
        if following:
            for k in range(1, dps - 1):
                hop(m + 1, k)
        project_out(m)
        if following:
            for k in range(dps - 1, dps):
                hop(m + 1, k)
        if following:
            for k in range(0, dps - 1):
                collect(m + 1, k)
        leave(m)
        if following and m + 2 < micros:
            enter_first(m + 2)

    for copy in started:
        copy.wait_send()
    for u in range(micros * parts):
        for owner in range(dps):
            for j in range(1, towers):
                tower_copy(u, owner, j).wait_send()

            @pl.when((dp_at >= owner) & (dp_at < dps - 1))
            def _():
                pass_on(u, owner, 1).wait_send()

            @pl.when((dp_at <= owner) & (dp_at > 0))
            def _():
                pass_on(u, owner, 0).wait_send()

    @pl.when(section_at < sections - 1)
    def _():
        for u in range(micros * parts):
            relays[u].wait_send()


def shards(stream, routes, tower_gain, qkv_weight, out_weight):
    micros, rows, width = stream.shape
    sections = lax.axis_size("section")
    dps = lax.axis_size("dp")
    towers = lax.axis_size("tower")
    head = qkv_weight.shape[-1]
    model = tower_gain.shape[-1]
    slots = rows // 2
    routed = towers * slots
    parts = 2
    units = micros * parts
    part = width // parts
    bf16 = jnp.bfloat16
    dma = pltpu.SemaphoreType.DMA
    vmem = pl.BlockSpec(memory_space=pltpu.VMEM)
    hbm = pl.BlockSpec(memory_space=pl.ANY)
    return pl.pallas_call(
        functools.partial(kernel, sections, dps, towers),
        out_shape=jax.ShapeDtypeStruct((1, micros, rows, width), bf16),
        in_specs=[hbm] * 5,
        out_specs=vmem,
        scratch_shapes=[
            pltpu.VMEM((model, 3 * head), bf16),
            pltpu.VMEM((dps * head, width), bf16),
            pltpu.VMEM((1, model), jnp.float32),
            pltpu.VMEM((micros, 1, rows), jnp.int32),
            pltpu.VMEM((towers, 8, 128), jnp.int32),
            pltpu.VMEM((micros, towers, towers, slots, rows), bf16),
            pltpu.VMEM((units, dps, rows, part), bf16),
            pltpu.VMEM((units, dps, towers, slots, part), bf16),
            pltpu.VMEM((units, dps, towers, slots, part), bf16),
            pltpu.VMEM((routed, 3 * head), jnp.float32),
            pltpu.VMEM((routed, 128), jnp.float32),
            pltpu.VMEM((micros, routed, head), bf16),
            pltpu.VMEM((micros, towers, slots, 2 * head), bf16),
            pltpu.VMEM((micros, towers, towers, slots, 2 * head), bf16),
            pltpu.VMEM((micros, routed, dps * head), bf16),
            pltpu.VMEM((units, towers, slots, part), bf16),
            pltpu.VMEM((units, towers, slots, part), bf16),
            dma((6 + units,)),
            dma((towers,)), dma((towers,)),
            dma((units, 2, dps)), dma((units, dps)),
            dma((units, dps, towers)), dma((units, dps, towers)),
            dma((micros, towers)), dma((micros, towers)),
            dma((micros, dps)), dma((micros, dps)),
            dma((units, towers)), dma((units, towers)),
            dma((units,)), dma((units,)),
        ],
        compiler_params=pltpu.CompilerParams(
            collective_id=0, has_side_effects=True, vmem_limit_bytes=60 * 1024 * 1024
        ),
        name="relay",
    )(
        stream,
        jnp.transpose(routes, (0, 2, 1)),
        tower_gain.reshape(1, model),
        jnp.transpose(qkv_weight.reshape(model, 3, head), (1, 0, 2)),
        out_weight.reshape(dps * head, width),
    )


def solution(mesh):
    placed = (
        P(None, "tower", "dp"),
        P(None, "tower", None),
        P("section", "tower", None),
        P("section", "tower", None, "dp", None, None),
        P("section", "tower", None, None, "dp"),
    )
    return jax.shard_map(
        shards,
        mesh=mesh,
        in_specs=placed,
        out_specs=P("section", None, "tower", "dp"),
        check_vma=False,
    )
```
